512 devices in a mesh: gx: 8 (over z), gy: 8 (over y_lo, x), gz: 8 (over y_hi, core).
Axes of the slice: x: 4, y: 8 (y_hi: 4, y_lo: 2; y = y_hi * 2 + y_lo), z: 8, core: 2. Of those that a mesh axis runs over, the one named last changes fastest.
Arguments:
- tokens: bfloat16 [2048, 8192], P('gy', ('gz', 'gx')), may hold values from -6 to 6
- gate_weight: bfloat16 [8192, 14336], P(('gz', 'gy'), 'gx'), may hold values from -0.0625 to 0.0625
- up_weight: bfloat16 [8192, 14336], P(('gz', 'gy'), 'gx'), may hold values from -0.0625 to 0.0625
- down_weight: bfloat16 [14336, 8192], P(('gx', 'gy'), 'gz'), may hold values from -0.046875 to 0.046875
Outputs:
- ffn_out: bfloat16 [2048, 8192], P('gy', ('gz', 'gx'))
The draws below stay inside these ranges and needn't reach their ends.
All inputs are finite; a program needn't handle non-finite values.
Results may differ from the reference program's by a relative error of at most 0.019.
Values may be sent and summed in bfloat16 or wider, within the bound.
A program may use at most 64 MiB of HBM per device.

```python
import jax
import jax.numpy as jnp

D = 8192
FF = 14336
TOKENS = 2048


def block_scale(stream_key, extent, pieces, least, top_value):
    def one(dim, blocks):
        steps = jax.random.uniform(jax.random.fold_in(jax.random.fold_in(stream_key, 6), dim), (blocks,), jnp.float32, least / len(pieces), top_value / len(pieces))
        return jnp.repeat(jnp.exp(steps), extent[dim] // blocks).reshape((-1,) + (1,) * (len(extent) - dim - 1))

    gain = one(*pieces[0])
    for cut in pieces[1:]:
        gain = gain * one(*cut)
    return gain


def gaussian(stream_key, extent, scale, reach, shards=(), held_as=jnp.bfloat16):
    entries = jax.random.normal(stream_key, extent, jnp.float32) * scale
    if len(shards) > 0:
        entries = block_scale(stream_key, extent, shards, -0.22, 0.18) * entries
    return jnp.clip(entries, min=-reach, max=reach).astype(held_as)


def setup_inputs(seed: int = 0) -> dict:
    keys = jax.random.split(jax.random.key(seed), 5)
    return {
        "tokens": gaussian(keys[0], (TOKENS, D), 1.0, 6.0, ((0, 8), (1, 64))),
        "gate_weight": gaussian(keys[1], (D, FF), D ** -0.5, 0.0625, ((0, 64), (1, 8))),
        "up_weight": gaussian(keys[2], (D, FF), D ** -0.5, 0.0625, ((0, 64), (1, 8))),
        "down_weight": gaussian(keys[3], (FF, D), FF ** -0.5, 0.046875, ((0, 64), (1, 8))),
    }


def reference(tokens, gate_weight, up_weight, down_weight):
    inputs = tokens.astype(jnp.float32)
    gate_sum = jnp.dot(inputs, gate_weight.astype(jnp.float32), preferred_element_type=jnp.float32)
    up_sum = jnp.dot(inputs, up_weight.astype(jnp.float32), preferred_element_type=jnp.float32)
    hidden = (jax.nn.silu(gate_sum) * up_sum).astype(jnp.bfloat16)
    output = jnp.dot(hidden.astype(jnp.float32), down_weight.astype(jnp.float32), preferred_element_type=jnp.float32)
    return output.astype(jnp.bfloat16)
```

```python
import functools

import jax
import jax.numpy as jnp
from jax import lax
from jax.experimental import pallas as pl
from jax.experimental.pallas import tpu as pltpu
from jax.sharding import PartitionSpec as P

MESH = pl.DeviceIdType.MESH
F32, BF16 = jnp.float32, jnp.bfloat16
CHUNKS = 7
HALF = 896
ROWS = 224


def device(x, y, z, c):
    return (z, (y % 2) * 4 + x, (y // 2) * 2 + c)


def remote(src, dst, send, recv, target):
    copy = pltpu.make_async_remote_copy(
        src_ref=src, dst_ref=dst, send_sem=send, recv_sem=recv, device_id=target, device_id_type=MESH
    )
    copy.start()


def wait(ref, sem):
    pltpu.make_async_copy(ref, ref, sem).wait()


def kernel(
    tok_in, gate_in, up_in, down_in, out_ref,
    tok, wbuf, cbuf, s1, r1, sb, rb, hid, dbuf, osend, orecv,
    tok_sem, x_send, x_recv, f_send, ch_send, ch_recv, h_send, h1, h2, hs_send, hs_recv, d_sem, o_sem,
):
    z = lax.axis_index("gx")
    gy, gz = lax.axis_index("gy"), lax.axis_index("gz")
    x, ylo, yhi, c = gy % 4, gy // 4, gz // 2, gz % 2
    y = yhi * 2 + ylo
    right, left = (x + 1) % 4, (x + 3) % 4
    sibling = device(x, y, z, 1 - c)

    def at_y(step):
        return device(x, (y + 8 + step) % 8, z, c)

    peers = [device(n, y, z, k) for n in (left, right) for k in (0, 1)]
    peers += [sibling] + [at_y(step) for step in (-2, -1, 1, 2)]
    other = 2 * yhi + 1 - ylo
    peers += [device(x, y, (z + dz) % 8, c) for dz in range(1, 8)]
    peers += [device(x, other, (z + dz) % 8, c) for dz in range(1, 8)]
    barrier = pltpu.get_barrier_semaphore()
    for peer in peers:
        pl.semaphore_signal(barrier, inc=1, device_id=peer, device_id_type=MESH)
    pl.semaphore_wait(barrier, len(peers))

    def x_own(j):
        rows = pl.ds(pl.multiple_of((c * 4 + x) * 128, 128), 128)
        for m, ref in enumerate((gate_in, up_in)):
            def part(core):
                return ref.at[:, pl.ds(pl.multiple_of(core * HALF + j * 128, 128), 128)]
            dst = wbuf.at[j, rows, pl.ds(m * 128, 128)]
            for core in (0, 1):
                remote(part(core), dst, x_send.at[j], x_recv.at[j, 2 * c], device(right, y, z, core))
                remote(part(core), dst, x_send.at[j], x_recv.at[j, 2 - c], device(left, y, z, core))
            remote(part(1 - c), dst, x_send.at[j], x_recv.at[j, 2], sibling)
            pltpu.make_async_copy(part(c), dst, x_recv.at[j, 2]).start()

    def x_forward(j):
        wait(wbuf.at[j, pl.ds(0, 128)], x_recv.at[j, 0])
        rows = pl.ds(pl.multiple_of(left * 128, 128), 128)
        block = wbuf.at[j, rows]
        remote(block, block, f_send.at[j], x_recv.at[j, 2], device(right, y, z, c))
        wait(wbuf.at[j, pl.ds(0, 128)], x_recv.at[j, 1])
        rows = pl.ds(pl.multiple_of((4 + right) * 128, 128), 128)
        block = wbuf.at[j, rows]
        remote(block, block, f_send.at[j], x_recv.at[j, 2], device(left, y, z, c))

    def own(j, step):
        rows = pl.ds(pl.multiple_of(((y + 8 + step) % 8) * 64, 64), 64)
        return cbuf[j, rows, :]

    def multiply(j):
        wait(wbuf.at[j, pl.ds(0, 768)], x_recv.at[j, 2])
        cbuf[j] = jnp.dot(tok[...], wbuf[j], preferred_element_type=F32)
        first = own(j, 4).astype(BF16)
        s1[j, 0] = first[:, :128]
        s1[j, 1] = first[:, 128:]
        for way, step in ((0, 1), (1, -1)):
            remote(s1.at[j, way], r1.at[j, way], ch_send.at[j, way, 0], ch_recv.at[j, way, 0], at_y(step))

    def pass_on(j, k):
        for way, step in ((0, 1), (1, -1)):
            mine = own(j, step * (4 - k))
            if k == 1:
                wait(r1.at[j, way], ch_recv.at[j, way, 0])
                part = r1[j, way].astype(F32)
                if way == 0:
                    sb[j, way, 0, :, :128] = (mine[:, :128] + part).astype(BF16)
                    sb[j, way, 0, :, 128:] = mine[:, 128:].astype(BF16)
                else:
                    sb[j, way, 0, :, :128] = mine[:, :128].astype(BF16)
                    sb[j, way, 0, :, 128:] = (mine[:, 128:] + part).astype(BF16)
            else:
                wait(rb.at[j, way, k - 2], ch_recv.at[j, way, k - 1])
                sb[j, way, k - 1] = (mine + rb[j, way, k - 2].astype(F32)).astype(BF16)
            remote(
                sb.at[j, way, k - 1], rb.at[j, way, k - 1], ch_send.at[j, way, k], ch_recv.at[j, way, k], at_y(step)
            )

    def tile(j):
        return pl.ds(pl.multiple_of(c * HALF + j * 128, 128), 128)

    def piece(j, step):
        return hid.at[pl.ds(pl.multiple_of(((y + 8 + step) % 8) * 64, 64), 64), tile(j)]

    def finish(j):
        for way in (0, 1):
            wait(rb.at[j, way, 2], ch_recv.at[j, way, 3])
        total = own(j, 0) + rb[j, 0, 2].astype(F32) + rb[j, 1, 2].astype(F32)
        gate, up = total[:, :128], total[:, 128:]
        value = gate / (1.0 + jnp.exp(-gate)) * up
        hid[pl.ds(pl.multiple_of(y * 64, 64), 64), tile(j)] = value.astype(BF16)
        remote(piece(j, 0), piece(j, 0), h_send.at[j], h1.at[j, 0], at_y(2))
        remote(piece(j, 0), piece(j, 0), h_send.at[j], h1.at[j, 1], at_y(-2))

    def relay(j):
        wait(piece(j, 0), h1.at[j, 0])
        for step in (2, 1, -1):
            remote(piece(j, -2), piece(j, -2), h_send.at[j], h2.at[j], at_y(step))
        wait(piece(j, 0), h1.at[j, 1])
        for step in (1, -1):
            remote(piece(j, 2), piece(j, 2), h_send.at[j], h2.at[j], at_y(step))

    def share(j):
        wait(hid.at[pl.ds(0, 320), pl.ds(0, 128)], h2.at[j])
        block = hid.at[:, tile(j)]
        remote(block, block, hs_send.at[j], hs_recv.at[j], sibling)

    def down_rows(k, at):
        return pl.ds(pl.multiple_of(k * HALF + at * ROWS, 16), ROWS)

    def down_pair():
        for k in range(4):
            cols = pl.ds(k * 128, 128)
            dst = dbuf.at[down_rows(ylo, x), cols]
            theirs = down_in.at[:, pl.ds(pl.multiple_of((2 * k + 1 - ylo) * 128, 128), 128)]
            remote(theirs, dst, d_sem.at[0], d_sem.at[1], device(x, other, z, c))
            ours = down_in.at[:, pl.ds(pl.multiple_of((2 * k + ylo) * 128, 128), 128)]
            pltpu.make_async_copy(ours, dst, d_sem.at[1]).start()

    def down_own():
        wait(dbuf.at[pl.ds(0, 2 * ROWS)], d_sem.at[1])
        for k in (0, 1):
            block = dbuf.at[down_rows(k, x)]
            remote(block, block, d_sem.at[2], d_sem.at[3 if k == 0 else 5], device(right, y, z, c))
            remote(block, block, d_sem.at[2], d_sem.at[4 if k == 1 else 5], device(left, y, z, c))

    def down_forward():
        wait(dbuf.at[pl.ds(0, ROWS)], d_sem.at[3])
        block = dbuf.at[down_rows(0, left)]
        remote(block, block, d_sem.at[6], d_sem.at[5], device(right, y, z, c))
        wait(dbuf.at[pl.ds(0, ROWS)], d_sem.at[4])
        block = dbuf.at[down_rows(1, right)]
        remote(block, block, d_sem.at[6], d_sem.at[5], device(left, y, z, c))

    x_own(0)
    x_own(1)
    plane = 2 * yhi + z // 4
    tok_dst = tok.at[
        pl.ds(pl.multiple_of(ylo * 256, 256), 256), pl.ds(pl.multiple_of(c * 512 + (z % 4) * 128, 128), 128)
    ]
    for dz in (4, 3, 5, 2, 6, 1, 7):
        remote(tok_in, tok_dst, tok_sem.at[0], tok_sem.at[1], device(x, plane, (z + dz) % 8, c))

    @pl.when(plane == y)
    def _():
        pltpu.make_async_copy(tok_in, tok_dst, tok_sem.at[1]).start()

    @pl.when(plane != y)
    def _():
        remote(tok_in, tok_dst, tok_sem.at[2], tok_sem.at[1], device(x, plane, z, c))

    down_pair()
    x_forward(0)
    x_own(2)
    x_forward(1)
    x_own(3)
    half = tok.at[:, pl.ds(pl.multiple_of(c * 512, 512), 512)]
    wait(half, tok_sem.at[1])
    remote(half, half, tok_sem.at[3], tok_sem.at[4], sibling)
    wait(half, tok_sem.at[4])

    def tick(t, carry):
        def when(lo, hi, f, *args):
            @pl.when((t >= lo) & (t < hi))
            def _():
                f(*args)

        when(0, CHUNKS - 2, lambda: x_forward(t + 2))
        when(0, CHUNKS - 4, lambda: x_own(t + 4))
        when(CHUNKS - 4, CHUNKS - 3, down_own)
        when(0, CHUNKS, lambda: multiply(t))
        when(1, CHUNKS + 1, lambda: pass_on(t - 1, 2))
        when(2, CHUNKS + 2, lambda: finish(t - 2))
        when(3, CHUNKS + 3, lambda: relay(t - 3))
        when(4, CHUNKS + 4, lambda: share(t - 4))
        when(CHUNKS + 1, CHUNKS + 2, down_forward)
        when(0, CHUNKS, lambda: pass_on(t, 1))
        when(1, CHUNKS + 1, lambda: pass_on(t - 1, 3))
        return carry

    lax.fori_loop(0, CHUNKS + 2, tick, 0)
    relay(CHUNKS - 1)
    share(CHUNKS - 2)
    share(CHUNKS - 1)
    wait(dbuf.at[pl.ds(0, 4 * ROWS)], d_sem.at[5])

    def shared(j, carry):
        wait(hid.at[:, pl.ds(0, 128)], hs_recv.at[j])
        return carry

    lax.fori_loop(0, CHUNKS, shared, 0)

    for t in (0, 1):
        rows = pl.ds(t * 256, 256)
        for n in (0, 1):
            block = jnp.dot(hid[rows, :], dbuf[:, n * 256 : n * 256 + 256], preferred_element_type=F32)
            block = block.astype(BF16)
            for k in (2 * n, 2 * n + 1):
                osend[t, k] = block[:, (k - 2 * n) * 128 : (k - 2 * n) * 128 + 128]
                at = 2 * k + ylo
                here = jnp.logical_and(at == z, ylo == t)

                @pl.when(here)
                def _():
                    pltpu.make_async_copy(osend.at[t, k], orecv.at[z], o_sem.at[1]).start()

                @pl.when(jnp.logical_not(here))
                def _():
                    remote(osend.at[t, k], orecv.at[z], o_sem.at[0], o_sem.at[1], device(x, 2 * yhi + t, at, c))

    wait(orecv, o_sem.at[1])
    total = orecv[0].astype(F32)
    for k in range(1, 8):
        total = total + orecv[k].astype(F32)
    out_ref[...] = total.astype(BF16)

    wait(orecv.at[pl.ds(0, 7)], o_sem.at[0])

    @pl.when(ylo != z % 2)
    def _():
        wait(orecv.at[0], o_sem.at[0])

    wait(orecv.at[pl.ds(0, 7)], tok_sem.at[0])

    @pl.when(plane != y)
    def _():
        wait(orecv.at[0], tok_sem.at[2])

    wait(half, tok_sem.at[3])
    wait(dbuf.at[pl.ds(0, ROWS)], d_sem.at[0])
    wait(dbuf.at[pl.ds(0, 4 * ROWS)], d_sem.at[2])
    wait(dbuf.at[pl.ds(0, 2 * ROWS)], d_sem.at[6])

    def drain(j, carry):
        wait(wbuf.at[j, pl.ds(0, 640)], x_send.at[j])
        wait(wbuf.at[j, pl.ds(0, 256)], f_send.at[j])
        for way in (0, 1):
            wait(s1.at[j, way], ch_send.at[j, way, 0])
            for k in (1, 2, 3):
                wait(sb.at[j, way, k - 1], ch_send.at[j, way, k])
        wait(hid.at[pl.ds(0, 448), pl.ds(0, 128)], h_send.at[j])
        wait(hid.at[:, pl.ds(0, 128)], hs_send.at[j])
        return carry

    lax.fori_loop(0, CHUNKS, drain, 0)


def local(tokens, gate_weight, up_weight, down_weight):
    dma = pltpu.SemaphoreType.DMA
    J = CHUNKS
    return pl.pallas_call(
        kernel,
        out_shape=jax.ShapeDtypeStruct((256, 128), BF16),
        in_specs=[pl.BlockSpec(memory_space=pl.ANY)] * 4,
        out_specs=pl.BlockSpec(memory_space=pltpu.VMEM),
        scratch_shapes=[
            pltpu.VMEM((512, 1024), BF16),
            pltpu.VMEM((J, 1024, 256), BF16),
            pltpu.VMEM((J, 512, 256), F32),
            pltpu.VMEM((J, 2, 64, 128), BF16),
            pltpu.VMEM((J, 2, 64, 128), BF16),
            pltpu.VMEM((J, 2, 3, 64, 256), BF16),
            pltpu.VMEM((J, 2, 3, 64, 256), BF16),
            pltpu.VMEM((512, 2 * HALF), BF16),
            pltpu.VMEM((2 * HALF, 512), BF16),
            pltpu.VMEM((2, 4, 256, 128), BF16),
            pltpu.VMEM((8, 256, 128), BF16),
            dma((5,)),
            dma((J,)),
            dma((J, 3)),
            dma((J,)),
            dma((J, 2, 4)),
            dma((J, 2, 4)),
            dma((J,)),
            dma((J, 2)),
            dma((J,)),
            dma((J,)),
            dma((J,)),
            dma((7,)),
            dma((2,)),
        ],
        compiler_params=pltpu.CompilerParams(
            collective_id=0, has_side_effects=True, vmem_limit_bytes=48 << 20
        ),
        cost_estimate=pl.CostEstimate(flops=2 * 1409286144, bytes_accessed=4 << 20, transcendentals=114688),
    )(tokens, gate_weight, up_weight, down_weight)


def solution(mesh):
    in_specs = (
        P("gy", ("gz", "gx")),
        P(("gz", "gy"), "gx"),
        P(("gz", "gy"), "gx"),
        P(("gx", "gy"), "gz"),
    )
    out_specs = P("gy", ("gz", "gx"))
    return jax.shard_map(local, mesh=mesh, in_specs=in_specs, out_specs=out_specs, check_vma=False)
```

```python
import functools

import jax
import jax.numpy as jnp
from jax import lax
from jax.experimental import pallas as pl
from jax.experimental.pallas import tpu as pltpu
from jax.sharding import PartitionSpec as P

MESH = pl.DeviceIdType.MESH
F32, BF16 = jnp.float32, jnp.bfloat16
CHUNKS = 7
HALF = 896
GROUPS = 4
LAG = 2
ROWS = 224


def device(x, y, z, c):
    return (z, (y % 2) * 4 + x, (y // 2) * 2 + c)


def remote(src, dst, send, recv, target):
    copy = pltpu.make_async_remote_copy(
        src_ref=src, dst_ref=dst, send_sem=send, recv_sem=recv, device_id=target, device_id_type=MESH
    )
    copy.start()


def wait(ref, sem):
    pltpu.make_async_copy(ref, ref, sem).wait()


def kernel(
    tok_in, gate_in, up_in, down_in, out_ref,
    tok, wbuf, cbuf, s1, r1, sb, rb, hid, dbuf, osend, orecv,
    tok_sem, t_recv, x_send, x_recv, f_send, ch_send, ch_recv, h_send, h1, h2, hs_send, hs_recv, d_sem, o_send, o_recv,
):
    z = lax.axis_index("gx")
    gy, gz = lax.axis_index("gy"), lax.axis_index("gz")
    x, ylo, yhi, c = gy % 4, gy // 4, gz // 2, gz % 2
    y = yhi * 2 + ylo
    right, left = (x + 1) % 4, (x + 3) % 4
    sibling = device(x, y, z, 1 - c)

    def at_y(step):
        return device(x, (y + 8 + step) % 8, z, c)

    peers = [device(n, y, z, k) for n in (left, right) for k in (0, 1)]
    peers += [sibling] + [at_y(step) for step in (-2, -1, 1, 2)]
    other = 2 * yhi + 1 - ylo
    peers += [device(x, y, (z + dz) % 8, c) for dz in range(1, 8)]
    peers += [device(x, other, (z + dz) % 8, c) for dz in range(1, 8)]
    barrier = pltpu.get_barrier_semaphore()
    for peer in peers:
        pl.semaphore_signal(barrier, inc=1, device_id=peer, device_id_type=MESH)
    pl.semaphore_wait(barrier, len(peers))

    def x_own(j):
        rows = pl.ds(pl.multiple_of((c * 4 + x) * 128, 128), 128)
        for m, ref in enumerate((gate_in, up_in)):
            def part(core):
                return ref.at[:, pl.ds(pl.multiple_of(core * HALF + j * 128, 128), 128)]
            dst = wbuf.at[j, rows, pl.ds(m * 128, 128)]
            for core in (0, 1):
                remote(part(core), dst, x_send.at[j], x_recv.at[j, 2 * c], device(right, y, z, core))
                remote(part(core), dst, x_send.at[j], x_recv.at[j, 2 - c], device(left, y, z, core))
            remote(part(1 - c), dst, x_send.at[j], x_recv.at[j, 2], sibling)
            pltpu.make_async_copy(part(c), dst, x_recv.at[j, 2]).start()

    def x_forward(j):
        wait(wbuf.at[j, pl.ds(0, 128)], x_recv.at[j, 0])
        rows = pl.ds(pl.multiple_of(left * 128, 128), 128)
        block = wbuf.at[j, rows]
        remote(block, block, f_send.at[j], x_recv.at[j, 2], device(right, y, z, c))
        wait(wbuf.at[j, pl.ds(0, 128)], x_recv.at[j, 1])
        rows = pl.ds(pl.multiple_of((4 + right) * 128, 128), 128)
        block = wbuf.at[j, rows]
        remote(block, block, f_send.at[j], x_recv.at[j, 2], device(left, y, z, c))

    def own(j, step):
        rows = pl.ds(pl.multiple_of(((y + 8 + step) % 8) * 64, 64), 64)
        return cbuf[j, rows, :]

    def multiply(j):
        wait(wbuf.at[j, pl.ds(0, 768)], x_recv.at[j, 2])
        cbuf[j] = jnp.dot(tok[ylo], wbuf[j], preferred_element_type=F32)
        first = own(j, 4).astype(BF16)
        s1[j, 0] = first[:, :128]
        s1[j, 1] = first[:, 128:]
        for way, step in ((0, 1), (1, -1)):
            remote(s1.at[j, way], r1.at[j, way], ch_send.at[j, way, 0], ch_recv.at[j, way, 0], at_y(step))

    def pass_on(j, k):
        for way, step in ((0, 1), (1, -1)):
            mine = own(j, step * (4 - k))
            if k == 1:
                wait(r1.at[j, way], ch_recv.at[j, way, 0])
                part = r1[j, way].astype(F32)
                if way == 0:
                    sb[j, way, 0, :, :128] = (mine[:, :128] + part).astype(BF16)
                    sb[j, way, 0, :, 128:] = mine[:, 128:].astype(BF16)
                else:
                    sb[j, way, 0, :, :128] = mine[:, :128].astype(BF16)
                    sb[j, way, 0, :, 128:] = (mine[:, 128:] + part).astype(BF16)
            else:
                wait(rb.at[j, way, k - 2], ch_recv.at[j, way, k - 1])
                sb[j, way, k - 1] = (mine + rb[j, way, k - 2].astype(F32)).astype(BF16)
            remote(
                sb.at[j, way, k - 1], rb.at[j, way, k - 1], ch_send.at[j, way, k], ch_recv.at[j, way, k], at_y(step)
            )

    def finish(j):
        for way in (0, 1):
            wait(rb.at[j, way, 2], ch_recv.at[j, way, 3])
        total = own(j, 0) + rb[j, 0, 2].astype(F32) + rb[j, 1, 2].astype(F32)
        gate, up = total[:, :128], total[:, 128:]
        value = (gate / (1.0 + jnp.exp(-gate)) * up).astype(BF16)
        for g in range(GROUPS):
            hid[g, pl.ds(pl.multiple_of(y * 16, 16), 16), pl.ds(pl.multiple_of(c * HALF + j * 128, 128), 128)] = (
                value[g * 16 : g * 16 + 16]
            )

    mine = pl.ds(pl.multiple_of(c * HALF, 128), HALF)

    def piece(g, step):
        return hid.at[g, pl.ds(pl.multiple_of(((y + 8 + step) % 8) * 16, 16), 16), mine]

    def spread(g):
        remote(piece(g, 0), piece(g, 0), h_send.at[g], h1.at[g, 0], at_y(2))
        remote(piece(g, 0), piece(g, 0), h_send.at[g], h1.at[g, 1], at_y(-2))

    def relay(g):
        wait(piece(g, 0), h1.at[g, 0])
        for step in (2, 1, -1):
            remote(piece(g, -2), piece(g, -2), h_send.at[g], h2.at[g], at_y(step))
        wait(piece(g, 0), h1.at[g, 1])
        for step in (1, -1):
            remote(piece(g, 2), piece(g, 2), h_send.at[g], h2.at[g], at_y(step))

    def share(g):
        wait(hid.at[0, pl.ds(0, 80), pl.ds(0, HALF)], h2.at[g])
        block = hid.at[g, :, mine]
        remote(block, block, hs_send.at[g], hs_recv.at[g], sibling)

    def down_rows(k, at):
        return pl.ds(pl.multiple_of(k * HALF + at * ROWS, 16), ROWS)

    def down_pair():
        for k in range(4):
            cols = pl.ds(k * 128, 128)
            dst = dbuf.at[down_rows(ylo, x), cols]
            theirs = down_in.at[:, pl.ds(pl.multiple_of((2 * k + 1 - ylo) * 128, 128), 128)]
            remote(theirs, dst, d_sem.at[0], d_sem.at[1], device(x, other, z, c))
            ours = down_in.at[:, pl.ds(pl.multiple_of((2 * k + ylo) * 128, 128), 128)]
            pltpu.make_async_copy(ours, dst, d_sem.at[1]).start()

    def down_own():
        wait(dbuf.at[pl.ds(0, 2 * ROWS)], d_sem.at[1])
        for k in (0, 1):
            block = dbuf.at[down_rows(k, x)]
            remote(block, block, d_sem.at[2], d_sem.at[3 if k == 0 else 5], device(right, y, z, c))
            remote(block, block, d_sem.at[2], d_sem.at[4 if k == 1 else 5], device(left, y, z, c))

    def down_forward():
        wait(dbuf.at[pl.ds(0, ROWS)], d_sem.at[3])
        block = dbuf.at[down_rows(0, left)]
        remote(block, block, d_sem.at[6], d_sem.at[5], device(right, y, z, c))
        wait(dbuf.at[pl.ds(0, ROWS)], d_sem.at[4])
        block = dbuf.at[down_rows(1, right)]
        remote(block, block, d_sem.at[6], d_sem.at[5], device(left, y, z, c))

    def tok_block(at):
        at = (z + 8 + at) % 8
        return tok.at[
            at // 4,
            pl.ds(pl.multiple_of(ylo * 256, 256), 256),
            pl.ds(pl.multiple_of(c * 512 + (at % 4) * 128, 128), 128),
        ]

    def at_z(step):
        return device(x, y, (z + 8 + step) % 8, c)

    def cross(src, at):
        @pl.when(((z + 8 + at) % 8) // 4 != ylo)
        def _():
            remote(src, tok_block(at), tok_sem.at[0], tok_sem.at[1], device(x, other, z, c))

    def tok_first():
        pltpu.make_async_copy(tok_in, tok_block(0), tok_sem.at[2]).start()
        remote(tok_in, tok_block(0), tok_sem.at[3], t_recv.at[0], at_z(2))
        remote(tok_in, tok_block(0), tok_sem.at[3], t_recv.at[1], at_z(-2))
        cross(tok_in, 0)

    def tok_relay():
        wait(tok_block(0), t_recv.at[0])
        for step, slot in ((-1, 2), (1, 3), (2, 4)):
            remote(tok_block(-2), tok_block(-2), tok_sem.at[4], t_recv.at[slot], at_z(step))
        cross(tok_block(-2), -2)
        wait(tok_block(0), t_recv.at[1])
        for step, slot in ((1, 5), (-1, 6)):
            remote(tok_block(2), tok_block(2), tok_sem.at[4], t_recv.at[slot], at_z(step))
        cross(tok_block(2), 2)

    def tok_rows(plane):
        return tok.at[
            ylo, pl.ds(pl.multiple_of(plane * 256, 256), 256), pl.ds(pl.multiple_of(c * 512, 512), 512)
        ]

    def tok_mid():
        for slot, at in ((2, -1), (5, 1), (3, -3), (6, 3), (4, -4)):
            wait(tok_block(0), t_recv.at[slot])
            cross(tok_block(at), at)
        wait(tok_block(0), tok_sem.at[2])
        remote(tok_rows(ylo), tok_rows(ylo), tok_sem.at[5], tok_sem.at[6], sibling)

    def tok_last():
        wait(tok_rows(0), tok_sem.at[1])
        remote(tok_rows(1 - ylo), tok_rows(1 - ylo), tok_sem.at[5], tok_sem.at[6], sibling)
        wait(tok.at[0, :, pl.ds(0, 512)], tok_sem.at[6])

    tok_first()
    x_own(0)
    x_own(1)
    down_pair()
    x_own(2)
    x_own(3)
    tok_relay()
    x_own(4)
    x_forward(0)
    x_own(5)
    tok_mid()
    x_own(6)
    x_forward(1)
    tok_last()
    x_forward(2)

    def tick(t, carry):
        def when(lo, hi, f):
            @pl.when((t >= lo) & (t < hi))
            def _():
                f()

        when(0, CHUNKS - 3, lambda: x_forward(t + 3))
        when(CHUNKS - 3, CHUNKS - 2, down_own)
        when(13, 14, down_forward)
        when(4 * LAG, CHUNKS + 4 * LAG, lambda: finish(t - 4 * LAG))
        when(3 * LAG, CHUNKS + 3 * LAG, lambda: pass_on(t - 3 * LAG, 3))
        when(2 * LAG, CHUNKS + 2 * LAG, lambda: pass_on(t - 2 * LAG, 2))
        when(LAG, CHUNKS + LAG, lambda: pass_on(t - LAG, 1))
        when(0, CHUNKS, lambda: multiply(t))
        return carry

    lax.fori_loop(0, CHUNKS + 4 * LAG, tick, 0)
    for g in range(GROUPS):
        spread(g)
    wait(dbuf.at[pl.ds(0, 4 * ROWS)], d_sem.at[5])

    def output(g):
        wait(hid.at[0, :, pl.ds(0, HALF)], hs_recv.at[g])
        for n in (0, 1):
            block = jnp.dot(hid[g], dbuf[:, n * 256 : n * 256 + 256], preferred_element_type=F32)
            osend[g, n] = block.astype(BF16)
            for i in (0, 1):
                for t in (0, 1):
                    at = 2 * (2 * n + i) + ylo
                    src = osend.at[g, n, pl.ds(t * 64, 64), pl.ds(i * 128, 128)]
                    here = jnp.logical_and(at == z, ylo == t)

                    @pl.when(here)
                    def _():
                        pltpu.make_async_copy(src, orecv.at[g, z], o_recv.at[g]).start()

                    @pl.when(jnp.logical_not(here))
                    def _():
                        remote(src, orecv.at[g, z], o_send.at[g], o_recv.at[g], device(x, 2 * yhi + t, at, c))

    def last(t, carry):
        def when(lo, f):
            @pl.when((t >= lo) & (t < lo + GROUPS))
            def _():
                f()

        when(0, lambda: relay(t))
        when(1, lambda: share(t - 1))
        when(2, lambda: output(t - 2))
        return carry

    lax.fori_loop(0, GROUPS + 2, last, 0)
    for g in range(GROUPS):
        wait(orecv.at[g], o_recv.at[g])
        total = orecv[g, 0].astype(F32)
        for k in range(1, 8):
            total = total + orecv[g, k].astype(F32)
        total = total.astype(BF16)
        for k in range(4):
            out_ref[k * 64 + g * 16 : k * 64 + g * 16 + 16, :] = total[k * 16 : k * 16 + 16]

    def left_late(g, carry):
        wait(orecv.at[0, pl.ds(0, 7)], o_send.at[g])

        @pl.when(ylo != z % 2)
        def _():
            wait(orecv.at[0, 0], o_send.at[g])

        wait(hid.at[0, pl.ds(0, 112), pl.ds(0, HALF)], h_send.at[g])
        wait(hid.at[0, :, pl.ds(0, HALF)], hs_send.at[g])
        return carry

    lax.fori_loop(0, GROUPS, left_late, 0)
    wait(tok.at[0, :, pl.ds(0, 256)], tok_sem.at[0])
    wait(tok.at[0, pl.ds(0, 256), pl.ds(0, 256)], tok_sem.at[3])
    wait(tok.at[0, pl.ds(0, 256), pl.ds(0, 640)], tok_sem.at[4])
    wait(tok.at[0, :, pl.ds(0, 512)], tok_sem.at[5])
    wait(dbuf.at[pl.ds(0, ROWS)], d_sem.at[0])
    wait(dbuf.at[pl.ds(0, 4 * ROWS)], d_sem.at[2])
    wait(dbuf.at[pl.ds(0, 2 * ROWS)], d_sem.at[6])

    def drain(j, carry):
        wait(wbuf.at[j, pl.ds(0, 640)], x_send.at[j])
        wait(wbuf.at[j, pl.ds(0, 256)], f_send.at[j])
        for way in (0, 1):
            wait(s1.at[j, way], ch_send.at[j, way, 0])
            for k in (1, 2, 3):
                wait(sb.at[j, way, k - 1], ch_send.at[j, way, k])
        return carry

    lax.fori_loop(0, CHUNKS, drain, 0)


def local(tokens, gate_weight, up_weight, down_weight):
    dma = pltpu.SemaphoreType.DMA
    J = CHUNKS
    return pl.pallas_call(
        kernel,
        out_shape=jax.ShapeDtypeStruct((256, 128), BF16),
        in_specs=[pl.BlockSpec(memory_space=pl.ANY)] * 4,
        out_specs=pl.BlockSpec(memory_space=pltpu.VMEM),
        scratch_shapes=[
            pltpu.VMEM((2, 512, 1024), BF16),
            pltpu.VMEM((J, 1024, 256), BF16),
            pltpu.VMEM((J, 512, 256), F32),
            pltpu.VMEM((J, 2, 64, 128), BF16),
            pltpu.VMEM((J, 2, 64, 128), BF16),
            pltpu.VMEM((J, 2, 3, 64, 256), BF16),
            pltpu.VMEM((J, 2, 3, 64, 256), BF16),
            pltpu.VMEM((GROUPS, 128, 2 * HALF), BF16),
            pltpu.VMEM((2 * HALF, 512), BF16),
            pltpu.VMEM((GROUPS, 2, 128, 256), BF16),
            pltpu.VMEM((GROUPS, 8, 64, 128), BF16),
            dma((7,)),
            dma((7,)),
            dma((J,)),
            dma((J, 3)),
            dma((J,)),
            dma((J, 2, 4)),
            dma((J, 2, 4)),
            dma((GROUPS,)),
            dma((GROUPS, 2)),
            dma((GROUPS,)),
            dma((GROUPS,)),
            dma((GROUPS,)),
            dma((7,)),
            dma((GROUPS,)),
            dma((GROUPS,)),
        ],
        compiler_params=pltpu.CompilerParams(
            collective_id=0, has_side_effects=True, vmem_limit_bytes=62 << 20
        ),
        cost_estimate=pl.CostEstimate(flops=2 * 1409286144, bytes_accessed=4 << 20, transcendentals=114688),
    )(tokens, gate_weight, up_weight, down_weight)


def solution(mesh):
    in_specs = (
        P("gy", ("gz", "gx")),
        P(("gz", "gy"), "gx"),
        P(("gz", "gy"), "gx"),
        P(("gx", "gy"), "gz"),
    )
    out_specs = P("gy", ("gz", "gx"))
    return jax.shard_map(local, mesh=mesh, in_specs=in_specs, out_specs=out_specs, check_vma=False)
```

```python
import functools

import jax
import jax.numpy as jnp
from jax import lax
from jax.experimental import pallas as pl
from jax.experimental.pallas import tpu as pltpu
from jax.sharding import PartitionSpec as P

MESH = pl.DeviceIdType.MESH
F32, BF16 = jnp.float32, jnp.bfloat16
CHUNKS = 7
HALF = 896
GROUPS = 4
LAG = 3
ROWS = 224


def device(x, y, z, c):
    return (z, (y % 2) * 4 + x, (y // 2) * 2 + c)


def remote(src, dst, send, recv, target):
    copy = pltpu.make_async_remote_copy(
        src_ref=src, dst_ref=dst, send_sem=send, recv_sem=recv, device_id=target, device_id_type=MESH
    )
    copy.start()


def wait(ref, sem):
    pltpu.make_async_copy(ref, ref, sem).wait()


def kernel(
    tok_in, gate_in, up_in, down_in, out_ref,
    tok, wbuf, cbuf, s1, r1, sb, rb, hid, dbuf, osend, orecv,
    tok_sem, t_recv, x_send, x_recv, f_send, ch_send, ch_recv, h_send, h1, h2, hs_send, hs_recv, d_sem, o_send, o_recv,
):
    z = lax.axis_index("gx")
    gy, gz = lax.axis_index("gy"), lax.axis_index("gz")
    x, ylo, yhi, c = gy % 4, gy // 4, gz // 2, gz % 2
    y = yhi * 2 + ylo
    right, left = (x + 1) % 4, (x + 3) % 4
    sibling = device(x, y, z, 1 - c)

    def at_y(step):
        return device(x, (y + 8 + step) % 8, z, c)

    peers = [device(n, y, z, k) for n in (left, right) for k in (0, 1)]
    peers += [sibling] + [at_y(step) for step in (-2, -1, 1, 2)]
    other = 2 * yhi + 1 - ylo
    peers += [device(x, y, (z + dz) % 8, c) for dz in range(1, 8)]
    peers += [device(x, other, (z + dz) % 8, c) for dz in range(1, 8)]
    barrier = pltpu.get_barrier_semaphore()
    for peer in peers:
        pl.semaphore_signal(barrier, inc=1, device_id=peer, device_id_type=MESH)
    pl.semaphore_wait(barrier, len(peers))

    def x_own(j):
        rows = pl.ds(pl.multiple_of((c * 4 + x) * 128, 128), 128)
        for m, ref in enumerate((gate_in, up_in)):
            def part(core):
                return ref.at[:, pl.ds(pl.multiple_of(core * HALF + j * 128, 128), 128)]
            dst = wbuf.at[j, rows, pl.ds(m * 128, 128)]
            for core in (0, 1):
                remote(part(core), dst, x_send.at[j], x_recv.at[j, 2 * c], device(right, y, z, core))
                remote(part(core), dst, x_send.at[j], x_recv.at[j, 2 - c], device(left, y, z, core))
            remote(part(1 - c), dst, x_send.at[j], x_recv.at[j, 2], sibling)
            pltpu.make_async_copy(part(c), dst, x_recv.at[j, 2]).start()

    def x_forward(j):
        wait(wbuf.at[j, pl.ds(0, 128)], x_recv.at[j, 0])
        rows = pl.ds(pl.multiple_of(left * 128, 128), 128)
        block = wbuf.at[j, rows]
        remote(block, block, f_send.at[j], x_recv.at[j, 2], device(right, y, z, c))
        wait(wbuf.at[j, pl.ds(0, 128)], x_recv.at[j, 1])
        rows = pl.ds(pl.multiple_of((4 + right) * 128, 128), 128)
        block = wbuf.at[j, rows]
        remote(block, block, f_send.at[j], x_recv.at[j, 2], device(left, y, z, c))

    def own(j, step):
        rows = pl.ds(pl.multiple_of(((y + 8 + step) % 8) * 64, 64), 64)
        return cbuf[j, rows, :]

    def multiply(j):
        wait(wbuf.at[j, pl.ds(0, 768)], x_recv.at[j, 2])
        cbuf[j] = jnp.dot(tok[ylo], wbuf[j], preferred_element_type=F32)
        first = own(j, 4).astype(BF16)
        s1[j, 0] = first[:, :128]
        s1[j, 1] = first[:, 128:]
        for way, step in ((0, 1), (1, -1)):
            remote(s1.at[j, way], r1.at[j, way], ch_send.at[j, way, 0], ch_recv.at[j, way, 0], at_y(step))

    def pass_on(j, k):
        for way, step in ((0, 1), (1, -1)):
            mine = own(j, step * (4 - k))
            if k == 1:
                wait(r1.at[j, way], ch_recv.at[j, way, 0])
                part = r1[j, way].astype(F32)
                if way == 0:
                    sb[j, way, 0, :, :128] = (mine[:, :128] + part).astype(BF16)
                    sb[j, way, 0, :, 128:] = mine[:, 128:].astype(BF16)
                else:
                    sb[j, way, 0, :, :128] = mine[:, :128].astype(BF16)
                    sb[j, way, 0, :, 128:] = (mine[:, 128:] + part).astype(BF16)
            else:
                wait(rb.at[j, way, k - 2], ch_recv.at[j, way, k - 1])
                sb[j, way, k - 1] = (mine + rb[j, way, k - 2].astype(F32)).astype(BF16)
            remote(
                sb.at[j, way, k - 1], rb.at[j, way, k - 1], ch_send.at[j, way, k], ch_recv.at[j, way, k], at_y(step)
            )

    def finish(j):
        for way in (0, 1):
            wait(rb.at[j, way, 2], ch_recv.at[j, way, 3])
        total = own(j, 0) + rb[j, 0, 2].astype(F32) + rb[j, 1, 2].astype(F32)
        gate, up = total[:, :128], total[:, 128:]
        value = (gate / (1.0 + jnp.exp(-gate)) * up).astype(BF16)
        for g in range(GROUPS):
            hid[g, pl.ds(pl.multiple_of(y * 16, 16), 16), pl.ds(pl.multiple_of(c * HALF + j * 128, 128), 128)] = (
                value[g * 16 : g * 16 + 16]
            )

    mine = pl.ds(pl.multiple_of(c * HALF, 128), HALF)

    def piece(g, step):
        return hid.at[g, pl.ds(pl.multiple_of(((y + 8 + step) % 8) * 16, 16), 16), mine]

    def spread(g):
        remote(piece(g, 0), piece(g, 0), h_send.at[g], h1.at[g, 0], at_y(2))
        remote(piece(g, 0), piece(g, 0), h_send.at[g], h1.at[g, 1], at_y(-2))

    def relay(g):
        far = 2 - 4 * c
        for way in (0, 1):
            wait(piece(g, 0), h1.at[g, way])
        remote(piece(g, -far), piece(g, -far), h_send.at[g], h2.at[g], at_y(far))
        for block in (-2, 2):
            for step in (1, -1):
                remote(piece(g, block), piece(g, block), h_send.at[g], h2.at[g], at_y(step))

    def share(g):
        wait(hid.at[0, pl.ds(0, 80), pl.ds(0, HALF)], h2.at[g])
        block = hid.at[g, :, mine]
        remote(block, block, hs_send.at[g], hs_recv.at[g], sibling)

    def down_rows(k, at):
        return pl.ds(pl.multiple_of(k * HALF + at * ROWS, 16), ROWS)

    def down_pair():
        for k in range(4):
            cols = pl.ds(k * 128, 128)
            dst = dbuf.at[down_rows(ylo, x), cols]
            theirs = down_in.at[:, pl.ds(pl.multiple_of((2 * k + 1 - ylo) * 128, 128), 128)]
            remote(theirs, dst, d_sem.at[0], d_sem.at[1], device(x, other, z, c))
            ours = down_in.at[:, pl.ds(pl.multiple_of((2 * k + ylo) * 128, 128), 128)]
            pltpu.make_async_copy(ours, dst, d_sem.at[1]).start()

    def down_own():
        wait(dbuf.at[pl.ds(0, 2 * ROWS)], d_sem.at[1])
        for k in (0, 1):
            block = dbuf.at[down_rows(k, x)]
            remote(block, block, d_sem.at[2], d_sem.at[3 if k == 0 else 5], device(right, y, z, c))
            remote(block, block, d_sem.at[2], d_sem.at[4 if k == 1 else 5], device(left, y, z, c))

    def down_forward():
        wait(dbuf.at[pl.ds(0, ROWS)], d_sem.at[3])
        block = dbuf.at[down_rows(0, left)]
        remote(block, block, d_sem.at[6], d_sem.at[5], device(right, y, z, c))
        wait(dbuf.at[pl.ds(0, ROWS)], d_sem.at[4])
        block = dbuf.at[down_rows(1, right)]
        remote(block, block, d_sem.at[6], d_sem.at[5], device(left, y, z, c))

    def tok_block(at):
        at = (z + 8 + at) % 8
        return tok.at[
            at // 4,
            pl.ds(pl.multiple_of(ylo * 256, 256), 256),
            pl.ds(pl.multiple_of(c * 512 + (at % 4) * 128, 128), 128),
        ]

    def at_z(step):
        return device(x, y, (z + 8 + step) % 8, c)

    def cross(src, at):
        @pl.when(((z + 8 + at) % 8) // 4 != ylo)
        def _():
            remote(src, tok_block(at), tok_sem.at[0], tok_sem.at[1], device(x, other, z, c))

    def tok_first():
        pltpu.make_async_copy(tok_in, tok_block(0), tok_sem.at[2]).start()
        remote(tok_in, tok_block(0), tok_sem.at[3], t_recv.at[0], at_z(2))
        remote(tok_in, tok_block(0), tok_sem.at[3], t_recv.at[1], at_z(-2))
        cross(tok_in, 0)

    def tok_relay():
        far = 2 - 4 * c
        for way in (0, 1):
            wait(tok_block(0), t_recv.at[way])
        remote(tok_block(-far), tok_block(-far), tok_sem.at[4], t_recv.at[4], at_z(far))
        for block, step, slot in ((-2, -1, 2), (2, 1, 5), (-2, 1, 3), (2, -1, 6)):
            remote(tok_block(block), tok_block(block), tok_sem.at[4], t_recv.at[slot], at_z(step))
        cross(tok_block(-2), -2)
        cross(tok_block(2), 2)

    def tok_rows(plane):
        return tok.at[
            ylo, pl.ds(pl.multiple_of(plane * 256, 256), 256), pl.ds(pl.multiple_of(c * 512, 512), 512)
        ]

    def tok_mid():
        for slot, at in ((2, -1), (5, 1), (3, -3), (6, 3), (4, -4)):
            wait(tok_block(0), t_recv.at[slot])
            cross(tok_block(at), at)
        wait(tok_block(0), tok_sem.at[2])
        remote(tok_rows(ylo), tok_rows(ylo), tok_sem.at[5], tok_sem.at[6], sibling)

    def tok_last():
        wait(tok_rows(0), tok_sem.at[1])
        remote(tok_rows(1 - ylo), tok_rows(1 - ylo), tok_sem.at[5], tok_sem.at[6], sibling)
        wait(tok.at[0, :, pl.ds(0, 512)], tok_sem.at[6])

    tok_first()
    x_own(0)
    x_own(1)
    down_pair()
    x_own(2)
    x_own(3)
    x_own(4)
    tok_relay()
    x_own(5)
    x_own(6)
    tok_mid()
    x_forward(0)
    tok_last()
    x_forward(1)
    x_forward(2)

    def tick(t, carry):
        def when(lo, hi, f):
            @pl.when((t >= lo) & (t < hi))
            def _():
                f()

        when(0, 4, lambda: x_forward(t + 3))
        when(CHUNKS - 3, CHUNKS - 2, down_own)
        when(17, 18, down_forward)
        when(4 * LAG, CHUNKS + 4 * LAG, lambda: finish(t - 4 * LAG))
        when(3 * LAG, CHUNKS + 3 * LAG, lambda: pass_on(t - 3 * LAG, 3))
        when(2 * LAG, CHUNKS + 2 * LAG, lambda: pass_on(t - 2 * LAG, 2))
        when(LAG, CHUNKS + LAG, lambda: pass_on(t - LAG, 1))
        when(0, CHUNKS, lambda: multiply(t))
        return carry

    lax.fori_loop(0, CHUNKS + 4 * LAG, tick, 0)
    for g in range(GROUPS):
        spread(g)
    wait(dbuf.at[pl.ds(0, 4 * ROWS)], d_sem.at[5])

    def output(g):
        wait(hid.at[0, :, pl.ds(0, HALF)], hs_recv.at[g])
        for n in (0, 1):
            block = jnp.dot(hid[g], dbuf[:, n * 256 : n * 256 + 256], preferred_element_type=F32)
            osend[g, n] = block.astype(BF16)
            for i in (0, 1):
                for t in (0, 1):
                    at = 2 * (2 * n + i) + ylo
                    src = osend.at[g, n, pl.ds(t * 64, 64), pl.ds(i * 128, 128)]
                    here = jnp.logical_and(at == z, ylo == t)

                    @pl.when(here)
                    def _():
                        pltpu.make_async_copy(src, orecv.at[g, z], o_recv.at[g]).start()

                    @pl.when(jnp.logical_not(here))
                    def _():
                        remote(src, orecv.at[g, z], o_send.at[g], o_recv.at[g], device(x, 2 * yhi + t, at, c))

    def last(t, carry):
        def when(lo, f):
            @pl.when((t >= lo) & (t < lo + GROUPS))
            def _():
                f()

        when(0, lambda: relay(t))
        when(1, lambda: share(t - 1))
        when(2, lambda: output(t - 2))
        return carry

    lax.fori_loop(0, GROUPS + 2, last, 0)
    for g in range(GROUPS):
        wait(orecv.at[g], o_recv.at[g])
        total = orecv[g, 0].astype(F32)
        for k in range(1, 8):
            total = total + orecv[g, k].astype(F32)
        total = total.astype(BF16)
        for k in range(4):
            out_ref[k * 64 + g * 16 : k * 64 + g * 16 + 16, :] = total[k * 16 : k * 16 + 16]

    def left_late(g, carry):
        wait(orecv.at[0, pl.ds(0, 7)], o_send.at[g])

        @pl.when(ylo != z % 2)
        def _():
            wait(orecv.at[0, 0], o_send.at[g])

        wait(hid.at[0, pl.ds(0, 112), pl.ds(0, HALF)], h_send.at[g])
        wait(hid.at[0, :, pl.ds(0, HALF)], hs_send.at[g])
        return carry

    lax.fori_loop(0, GROUPS, left_late, 0)
    wait(tok.at[0, :, pl.ds(0, 256)], tok_sem.at[0])
    wait(tok.at[0, pl.ds(0, 256), pl.ds(0, 256)], tok_sem.at[3])
    wait(tok.at[0, pl.ds(0, 256), pl.ds(0, 640)], tok_sem.at[4])
    wait(tok.at[0, :, pl.ds(0, 512)], tok_sem.at[5])
    wait(dbuf.at[pl.ds(0, ROWS)], d_sem.at[0])
    wait(dbuf.at[pl.ds(0, 4 * ROWS)], d_sem.at[2])
    wait(dbuf.at[pl.ds(0, 2 * ROWS)], d_sem.at[6])

    def drain(j, carry):
        wait(wbuf.at[j, pl.ds(0, 640)], x_send.at[j])
        wait(wbuf.at[j, pl.ds(0, 256)], f_send.at[j])
        for way in (0, 1):
            wait(s1.at[j, way], ch_send.at[j, way, 0])
            for k in (1, 2, 3):
                wait(sb.at[j, way, k - 1], ch_send.at[j, way, k])
        return carry

    lax.fori_loop(0, CHUNKS, drain, 0)


def local(tokens, gate_weight, up_weight, down_weight):
    dma = pltpu.SemaphoreType.DMA
    J = CHUNKS
    return pl.pallas_call(
        kernel,
        out_shape=jax.ShapeDtypeStruct((256, 128), BF16),
        in_specs=[pl.BlockSpec(memory_space=pl.ANY)] * 4,
        out_specs=pl.BlockSpec(memory_space=pltpu.VMEM),
        scratch_shapes=[
            pltpu.VMEM((2, 512, 1024), BF16),
            pltpu.VMEM((J, 1024, 256), BF16),
            pltpu.VMEM((J, 512, 256), F32),
            pltpu.VMEM((J, 2, 64, 128), BF16),
            pltpu.VMEM((J, 2, 64, 128), BF16),
            pltpu.VMEM((J, 2, 3, 64, 256), BF16),
            pltpu.VMEM((J, 2, 3, 64, 256), BF16),
            pltpu.VMEM((GROUPS, 128, 2 * HALF), BF16),
            pltpu.VMEM((2 * HALF, 512), BF16),
            pltpu.VMEM((GROUPS, 2, 128, 256), BF16),
            pltpu.VMEM((GROUPS, 8, 64, 128), BF16),
            dma((7,)),
            dma((7,)),
            dma((J,)),
            dma((J, 3)),
            dma((J,)),
            dma((J, 2, 4)),
            dma((J, 2, 4)),
            dma((GROUPS,)),
            dma((GROUPS, 2)),
            dma((GROUPS,)),
            dma((GROUPS,)),
            dma((GROUPS,)),
            dma((7,)),
            dma((GROUPS,)),
            dma((GROUPS,)),
        ],
        compiler_params=pltpu.CompilerParams(
            collective_id=0, has_side_effects=True, vmem_limit_bytes=62 << 20
        ),
        cost_estimate=pl.CostEstimate(flops=2 * 1409286144, bytes_accessed=4 << 20, transcendentals=114688),
    )(tokens, gate_weight, up_weight, down_weight)


def solution(mesh):
    in_specs = (
        P("gy", ("gz", "gx")),
        P(("gz", "gy"), "gx"),
        P(("gz", "gy"), "gx"),
        P(("gx", "gy"), "gz"),
    )
    out_specs = P("gy", ("gz", "gx"))
    return jax.shard_map(local, mesh=mesh, in_specs=in_specs, out_specs=out_specs, check_vma=False)
```
